32 devices in a mesh: beam: 4 (over x, core), row: 8 (over z, y).
Axes of the slice: x: 2, y: 2, z: 4, core: 2. Of those that a mesh axis runs over, the one named last changes fastest.
Arguments:
- x_in: bfloat16 [4, 2, 16, 8192], P(None, None, None, 'beam'), may hold values from -6 to 6
- w_inner: bfloat16 [8192, 2, 16384], P('beam', None, 'row'), may hold values from -0.0625 to 0.0625
- w_bc: bfloat16 [8192, 2, 2048], P('beam', None, 'row'), may hold values from -0.0625 to 0.0625
- w_dt: bfloat16 [8192, 256], P('beam', 'row'), may hold values from -0.0625 to 0.0625
- conv_x_w: bfloat16 [4, 16384], P(None, 'row'), may hold values from -3 to 3
- conv_bc_w: bfloat16 [4, 2, 2048], P(None, None, 'row'), may hold values from -3 to 3
- dt_bias: float32 [256], P('row'), may hold values from -4 to 1
- a_log: float32 [256], P('row'), may hold values from 0 to 2.8
- d_skip: float32 [256], P('row'), may hold values from 0.5 to 2
- norm_gain: float32 [16384], P('row'), may hold values from 0.1 to 1.9
- w_out: bfloat16 [16384, 8192], P('row', 'beam'), may hold values from -0.046875 to 0.046875
- ssm_state: bfloat16 [2, 16, 256, 64, 256], P(None, 'beam', 'row'), may hold values from -6 to 6
- conv_x_state: bfloat16 [2, 16, 256, 64, 3], P(None, 'beam', 'row'), may hold values from -6 to 6
- conv_bc_state: bfloat16 [2, 16, 3, 2, 2048], P(None, 'beam', None, None, 'row'), may hold values from -6 to 6
- parents: int32 [4, 2, 16], replicated, may hold values from 0 to 15
Outputs:
- layer_out: bfloat16 [4, 32, 8192], P(None, 'row', 'beam')
- ssm_final: bfloat16 [2, 16, 256, 64, 256], P(None, 'beam', 'row')
- conv_x_final: bfloat16 [2, 16, 256, 64, 3], P(None, 'beam', 'row')
- conv_bc_final: bfloat16 [2, 16, 3, 2, 2048], P(None, 'beam', None, None, 'row')
The draws below stay inside these ranges and needn't reach their ends.
All inputs are finite; a program needn't handle non-finite values.
Results may differ from the reference program's by a relative error of at most 0.0077.
Values may be sent and summed in bfloat16 or wider, within the bound.
A program may use at most 192 MiB of HBM per device.

```python
import jax
import jax.numpy as jnp
from jax import lax

D = 8192
HEADS = 256
HDIM = 64
NSTATE = 256
GROUPS = 8
CONV = 4
BEAM_WIDTH = 16
SESS = 2
STEPS = 4
INNER = 16384
GN = 2048
BEAMS = 32


def plant(values, key, smallest, top_value):
    longest = values.shape.index(max(values.shape))
    spots = []
    for shift in (0, 1):
        where = [jax.random.randint(jax.random.fold_in(key, axis), (), 0, length) for axis, length in enumerate(values.shape)]
        where[longest] = (where[longest] + shift) % values.shape[longest]
        spots.append(tuple(where))
    return values.at[spots[0]].set(smallest).at[spots[1]].set(top_value)


def level_of(rng, extent, shards, smallest, top_value):
    level, own = 1.0, jax.random.fold_in(rng, 6)
    for axis_at, parts in shards:
        draws = jnp.exp(jax.random.uniform(jax.random.fold_in(own, axis_at), (parts,), jnp.float32, smallest / len(shards), top_value / len(shards)))
        level = level * jnp.repeat(draws, extent[axis_at] // parts).reshape([-1 if axis == axis_at else 1 for axis in range(len(extent))])
    return level


def noise(key, extent, scale, limit, pieces=(), dtype=jnp.bfloat16):
    values = jax.random.normal(key, extent, jnp.float32) * scale
    if len(pieces) > 0:
        values = level_of(key, extent, pieces, -0.22, 0.18) * values
    return jnp.clip(values, min=-limit, max=limit).astype(dtype)


def setup_inputs(seed: int = 0) -> dict:
    key_list = jax.random.split(jax.random.key(seed), 16)
    return {
        "x_in": noise(key_list[0], (STEPS, SESS, BEAM_WIDTH, D), 1.0, 6.0, ((3, 4),)),
        "w_inner": noise(key_list[1], (D, 2, INNER), D ** -0.5, 0.0625, ((0, 4), (2, 8))),
        "w_bc": noise(key_list[2], (D, 2, GN), D ** -0.5, 0.0625, ((0, 4), (2, 8))),
        "w_dt": noise(key_list[3], (D, HEADS), D ** -0.5, 0.0625, ((0, 4), (1, 8))),
        "conv_x_w": noise(key_list[4], (CONV, INNER), CONV ** -0.5, 3.0, ((1, 8),)),
        "conv_bc_w": noise(key_list[5], (CONV, 2, GN), CONV ** -0.5, 3.0, ((2, 8),)),
        "dt_bias": jnp.clip(-4.0 + 5.0 * jax.random.uniform(key_list[6], (HEADS,), jnp.float32) ** level_of(key_list[6], (HEADS,), ((0, 8),), -0.2, 0.2), -4.0, 1.0),
        "a_log": jnp.clip(2.8 * jax.random.uniform(key_list[7], (HEADS,), jnp.float32) ** level_of(key_list[7], (HEADS,), ((0, 8),), -0.2, 0.2), 0.0, 2.8),
        "d_skip": jnp.clip(0.5 + 1.5 * jax.random.uniform(key_list[8], (HEADS,), jnp.float32) ** level_of(key_list[8], (HEADS,), ((0, 8),), -0.2, 0.2), 0.5, 2.0),
        "norm_gain": jnp.clip(1.0 + 0.18 * jax.random.normal(key_list[9], (INNER,), jnp.float32), 0.1, 1.9),
        "w_out": noise(key_list[10], (INNER, D), INNER ** -0.5, 0.046875, ((0, 8), (1, 4))),
        "ssm_state": noise(key_list[11], (SESS, BEAM_WIDTH, HEADS, HDIM, NSTATE), 1.0, 6.0, ((1, 4), (2, 8))),
        "conv_x_state": noise(key_list[12], (SESS, BEAM_WIDTH, HEADS, HDIM, CONV - 1), 1.0, 6.0, ((1, 4), (2, 8))),
        "conv_bc_state": noise(key_list[13], (SESS, BEAM_WIDTH, CONV - 1, 2, GN), 1.0, 6.0, ((1, 4), (4, 8))),
        "parents": plant(jax.random.randint(key_list[14], (STEPS, SESS, BEAM_WIDTH), 0, BEAM_WIDTH), jax.random.fold_in(key_list[14], 1), 0, BEAM_WIDTH - 1).astype(jnp.int32),
    }


EPS = 1e-05

def stored(value):
    return lax.optimization_barrier(value.astype(jnp.bfloat16))

def reference(x_in, w_inner, w_bc, w_dt, conv_x_w, conv_bc_w, dt_bias, a_log, d_skip, norm_gain, w_out, ssm_state, conv_x_state, conv_bc_state, parents):
    group_heads = HEADS // GROUPS
    ssm_held = ssm_state
    conv_held = conv_x_state
    rim_held = conv_bc_state
    conv_taps = conv_x_w.astype(jnp.float32).reshape(CONV, HEADS, HDIM)
    bc_taps = conv_bc_w.astype(jnp.float32)
    decay_rates = jnp.exp(a_log.astype(jnp.float32))
    gains = norm_gain.astype(jnp.float32).reshape(HEADS, HDIM)
    picker = jax.vmap(lambda held, chosen: held[chosen])
    outputs = []
    for step in range(STEPS):
        parent = parents[step]
        ssm_held = picker(ssm_held, parent)
        conv_held = picker(conv_held, parent)
        rim_held = picker(rim_held, parent)
        tokens = x_in[step].reshape(BEAMS, D)
        inner = stored(jnp.dot(tokens, w_inner.reshape(D, 2 * INNER), preferred_element_type=jnp.float32))
        inner = inner.reshape(SESS, BEAM_WIDTH, 2, HEADS, HDIM)
        gate_in = inner[:, :, 0]
        x_new = inner[:, :, 1]
        bc_new = stored(jnp.dot(tokens, w_bc.reshape(D, 2 * GN), preferred_element_type=jnp.float32))
        bc_new = bc_new.reshape(SESS, BEAM_WIDTH, 2, GN)
        dt_raw = stored(jnp.dot(tokens, w_dt, preferred_element_type=jnp.float32)).reshape(SESS, BEAM_WIDTH, HEADS)
        mixed = lax.optimization_barrier(jnp.sum(conv_held.astype(jnp.float32) * jnp.transpose(conv_taps[:-1], (1, 2, 0)), axis=-1))
        mixed = mixed + conv_taps[-1] * x_new.astype(jnp.float32)
        x_conv = stored(jax.nn.silu(mixed))
        conv_held = jnp.concatenate([conv_held[..., 1:], x_new[..., None]], axis=-1)
        mixed_bc = lax.optimization_barrier(jnp.sum(rim_held.astype(jnp.float32) * bc_taps[:-1], axis=2)) + bc_taps[-1] * bc_new.astype(jnp.float32)
        bc_conv = stored(jax.nn.silu(mixed_bc))
        rim_held = jnp.concatenate([rim_held[:, :, 1:], bc_new[:, :, None]], axis=2)
        b_in = jnp.repeat(bc_conv[:, :, 0].reshape(SESS, BEAM_WIDTH, GROUPS, NSTATE), group_heads, axis=2).astype(jnp.float32)
        c_out = jnp.repeat(bc_conv[:, :, 1].reshape(SESS, BEAM_WIDTH, GROUPS, NSTATE), group_heads, axis=2).astype(jnp.float32)
        step_size = jax.nn.softplus(dt_raw.astype(jnp.float32) + dt_bias.astype(jnp.float32))
        decay = jnp.exp(-decay_rates * step_size)
        x_val = x_conv.astype(jnp.float32)
        state = decay[..., None, None] * ssm_held.astype(jnp.float32) + (step_size[..., None] * x_val)[..., None] * b_in[:, :, :, None, :]
        read = lax.optimization_barrier(jnp.sum(state * c_out[:, :, :, None, :], axis=-1)) + d_skip.astype(jnp.float32)[:, None] * x_val
        ssm_held = stored(state)
        gated = read * jax.nn.silu(gate_in.astype(jnp.float32))
        grouped = gated.reshape(SESS, BEAM_WIDTH, GROUPS, group_heads * HDIM)
        mean_sq = lax.optimization_barrier(jnp.sum(grouped * grouped, axis=-1, keepdims=True)) / (group_heads * HDIM)
        scaled = (grouped * lax.rsqrt(mean_sq + EPS)).reshape(SESS, BEAM_WIDTH, HEADS, HDIM)
        normed = stored(scaled * gains)
        result = jnp.dot(normed.reshape(BEAMS, INNER), w_out, preferred_element_type=jnp.float32).astype(jnp.bfloat16)
        outputs.append(result)
    return (jnp.stack(outputs), ssm_held, conv_held, rim_held)
```

```python
import functools

import jax
import jax.numpy as jnp
from jax import lax
from jax.experimental import pallas as pl
from jax.experimental.pallas import tpu as pltpu
from jax.sharding import PartitionSpec as P

HEADS = 256
GROUPS = 8
EPS = 1e-05
MIB = 1 << 20
F32 = jnp.float32
BF16 = jnp.bfloat16


def partner_2(shard, axis, stride):
    return lax.ppermute(shard, axis, [(i, i ^ 1 << stride) for i in range(lax.axis_size(axis))])


def project_kernel(x_ref, w_ref, bc_ref, out_ref, out_bc_ref):
    tokens, depth = x_ref.shape
    row = lax.broadcasted_iota(jnp.int32, (depth, 2 * depth), 0)
    col = lax.broadcasted_iota(jnp.int32, (depth, 2 * depth), 1)
    x = x_ref[...]
    first = jnp.dot(x, (col == 2 * row).astype(BF16), preferred_element_type=F32).astype(BF16)
    second = jnp.dot(x, (col == 2 * row + 1).astype(BF16), preferred_element_type=F32).astype(BF16)
    spread = jnp.concatenate([first, second], axis=0)

    @pl.when(pl.program_id(0) == 0)
    def _():
        out_ref[...] = jnp.zeros_like(out_ref)
        out_bc_ref[...] = jnp.zeros_like(out_bc_ref)

    w = w_ref[...].reshape(2 * depth, w_ref.shape[2])
    bc = bc_ref[...].reshape(2 * depth, bc_ref.shape[2])
    out_ref[...] += jnp.dot(spread, w, preferred_element_type=F32)
    out_bc_ref[...] += jnp.dot(spread, bc, preferred_element_type=F32)


def project(x, w, w_bc):
    tokens, width = x.shape
    depth = 256
    columns, columns_bc = w.shape[2], w_bc.shape[2]
    return pl.pallas_call(
        project_kernel,
        grid=(width // depth,),
        in_specs=[
            pl.BlockSpec((tokens, depth), lambda i: (0, i)),
            pl.BlockSpec((depth, 2, columns), lambda i: (i, 0, 0)),
            pl.BlockSpec((depth, 2, columns_bc), lambda i: (i, 0, 0)),
        ],
        out_specs=[
            pl.BlockSpec((2 * tokens, columns), lambda i: (0, 0)),
            pl.BlockSpec((2 * tokens, columns_bc), lambda i: (0, 0)),
        ],
        out_shape=[
            jax.ShapeDtypeStruct((2 * tokens, columns), F32),
            jax.ShapeDtypeStruct((2 * tokens, columns_bc), F32),
        ],
        compiler_params=pltpu.CompilerParams(vmem_limit_bytes=40 * MIB),
        cost_estimate=pl.CostEstimate(
            flops=8 * tokens * width * columns,
            bytes_accessed=4 * width * columns,
            transcendentals=0,
        ),
        name="project",
    )(x, w, w_bc)


def pick_kernel(where_ref, held_ref, out_ref):
    out_ref[...] = held_ref[...]


def pick(where, held):
    count = where.shape[0]
    _, rows, columns = held.shape
    return pl.pallas_call(
        pick_kernel,
        grid_spec=pltpu.PrefetchScalarGridSpec(
            num_scalar_prefetch=1,
            grid=(count,),
            in_specs=[pl.BlockSpec((1, rows, columns), lambda i, where: (where[i], 0, 0))],
            out_specs=pl.BlockSpec((1, rows, columns), lambda i, where: (i, 0, 0)),
        ),
        out_shape=jax.ShapeDtypeStruct((count, rows, columns), held.dtype),
        compiler_params=pltpu.CompilerParams(vmem_limit_bytes=16 * MIB),
        name="pick",
    )(where, held)


def read_kernel(c_ref, held_ref, out_ref):
    part = lax.dot_general(
        c_ref[0], held_ref[0], (((1,), (1,)), ((), ())), preferred_element_type=F32
    )

    @pl.when(pl.program_id(1) == 0)
    def _():
        out_ref[0] = part

    @pl.when(pl.program_id(1) > 0)
    def _():
        out_ref[0] += part


def read_held(c_masked, held, sessions):
    blocks, tokens, size = c_masked.shape
    rows = held.shape[1]
    beams = blocks // sessions
    return pl.pallas_call(
        read_kernel,
        grid=(sessions, beams),
        in_specs=[
            pl.BlockSpec((1, tokens, size), lambda s, j: (s * beams + j, 0, 0)),
            pl.BlockSpec((1, rows, size), lambda s, j: (s * beams + j, 0, 0)),
        ],
        out_specs=pl.BlockSpec((1, tokens, rows), lambda s, j: (s, 0, 0)),
        out_shape=jax.ShapeDtypeStruct((sessions, tokens, rows), F32),
        compiler_params=pltpu.CompilerParams(vmem_limit_bytes=16 * MIB),
        cost_estimate=pl.CostEstimate(
            flops=2 * blocks * tokens * size * rows,
            bytes_accessed=2 * blocks * rows * size,
            transcendentals=0,
        ),
        name="read_held",
    )(c_masked, held)


def final_kernel(count, which_ref, where_ref, left_ref, right_ref, *refs):
    held_refs, out_ref = refs[:-1], refs[-1]
    size = out_ref.shape[2]
    both = lax.dot_general(
        left_ref[0], right_ref[0], (((0,), (0,)), ((), ())), preferred_element_type=F32
    )
    which = which_ref[pl.program_id(0)]
    for piece, held_ref in enumerate(held_refs):

        @pl.when(which == piece)
        def _(held_ref=held_ref):
            state = both[:, size:] * held_ref[0].astype(F32) + both[:, :size]
            out_ref[0] = state.astype(out_ref.dtype)


def final_state(which, where, left, right, pieces):
    count, terms, rows = left.shape
    size = pieces[0].shape[2]
    chunk = min(rows, 1024)
    chunks = rows // chunk

    def place(piece, i, k, which, where):
        block = jnp.where(which[i] == piece, k, chunks - 1)
        return where[piece * count + i], block, 0

    return pl.pallas_call(
        functools.partial(final_kernel, count),
        grid_spec=pltpu.PrefetchScalarGridSpec(
            num_scalar_prefetch=2,
            grid=(count, chunks),
            in_specs=[
                pl.BlockSpec((1, terms, chunk), lambda i, k, which, where: (i, 0, k)),
                pl.BlockSpec((1, terms, 2 * size), lambda i, k, which, where: (i, 0, 0)),
            ]
            + [
                pl.BlockSpec((1, chunk, size), functools.partial(place, piece))
                for piece in range(len(pieces))
            ],
            out_specs=pl.BlockSpec((1, chunk, size), lambda i, k, which, where: (i, k, 0)),
        ),
        out_shape=jax.ShapeDtypeStruct((count, rows, size), BF16),
        compiler_params=pltpu.CompilerParams(vmem_limit_bytes=32 * MIB),
        name="final_state",
    )(which, where.reshape(-1), left, right, *pieces)


def exchange_kernel(axis, count, gather, x_ref, out_ref, got, done, *sems):
    me = lax.axis_index(axis)
    peers = [lax.rem(me + hop, count) for hop in range(1, count)]
    barrier = pltpu.get_barrier_semaphore()
    for peer in peers:
        pl.semaphore_signal(
            barrier, inc=1, device_id={axis: peer}, device_id_type=pl.DeviceIdType.MESH
        )
    pl.semaphore_wait(barrier, count - 1)

    def send(src, dst, hop, sent, landed):
        copy = pltpu.make_async_remote_copy(
            src_ref=src,
            dst_ref=dst,
            send_sem=sent.at[hop],
            recv_sem=landed.at[hop],
            device_id={axis: peers[hop]},
            device_id_type=pl.DeviceIdType.MESH,
        )
        copy.start()
        return copy

    copies = [
        send(x_ref.at[peer], got.at[hop], hop, sems[0], sems[1]) for hop, peer in enumerate(peers)
    ]
    total = x_ref[me].astype(F32)
    for hop, copy in enumerate(copies):
        copy.wait()
        total = total + got[hop].astype(F32)
    if not gather:
        out_ref[...] = total.astype(out_ref.dtype)
        return
    done[me] = total.astype(done.dtype)
    copies = [send(done.at[me], done.at[me], hop, sems[2], sems[3]) for hop in range(count - 1)]
    for copy in copies:
        copy.wait()
    out_ref[...] = done[...]


def exchange(x, axis, gather, collective_id, name):
    count, rows, columns = x.shape
    shape = (count, rows, columns) if gather else (rows, columns)
    sems = [pltpu.SemaphoreType.DMA((count - 1,)) for _ in range(4)]
    return pl.pallas_call(
        functools.partial(exchange_kernel, axis, count, gather),
        out_shape=jax.ShapeDtypeStruct(shape, BF16),
        in_specs=[pl.BlockSpec(memory_space=pltpu.VMEM)],
        out_specs=pl.BlockSpec(memory_space=pltpu.VMEM),
        scratch_shapes=[
            pltpu.VMEM((count - 1, rows, columns), x.dtype),
            pltpu.VMEM((count, rows, columns) if gather else (1, 16, 128), BF16),
        ]
        + sems,
        compiler_params=pltpu.CompilerParams(
            collective_id=collective_id, has_side_effects=True, vmem_limit_bytes=32 * MIB
        ),
        name=name,
    )(x)


def split(value, pieces):
    out = []
    for _ in range(pieces):
        piece = value.astype(BF16)
        out.append(piece)
        value = value - piece.astype(F32)
    return out


def onehot(index, size, dtype):
    return (index[..., None] == jnp.arange(size, dtype=jnp.int32)).astype(dtype)


def choose(selector, values):
    extra = values.ndim - 2
    sel = selector.reshape(selector.shape + (1,) * extra)
    return jnp.sum(jnp.where(sel, values[:, None], 0), axis=2)


def run(
    slots_per_device,
    x_in,
    w_inner,
    w_bc,
    w_dt,
    conv_w,
    dt_bias,
    a_log,
    d_skip,
    norm_gain,
    w_out,
    held,
    conv_held,
    history,
    needed,
    rank,
    parents,
):
    beam_index = lax.axis_index("beam")
    row_index = lax.axis_index("row")
    steps, sessions, width, d_local = x_in.shape
    beams = lax.axis_size("beam")
    local_beams = width // beams
    held_count, channels, size = held.shape
    heads_local = w_dt.shape[1]
    head_dim = channels // heads_local
    tap_count = conv_w.shape[0]
    group_heads = HEADS // GROUPS
    group_span = lax.axis_size("row") // GROUPS
    bc_local = w_bc.shape[2]
    sources = (tap_count - 1 + steps) * width
    tokens = steps * width

    own_needed = lax.dynamic_index_in_dim(needed, beam_index, 0, keepdims=False)
    own_rank = lax.dynamic_index_in_dim(rank, beam_index, 0, keepdims=False)
    slot_ids = jnp.arange(slots_per_device, dtype=jnp.int32)
    in_slot = own_needed[None, :] & (own_rank[None, :] == slot_ids[:, None])
    slot_from = jnp.sum(
        jnp.where(in_slot, jnp.arange(held_count, dtype=jnp.int32)[None, :], 0), axis=1
    ).astype(jnp.int32)
    x_all = x_in.reshape(steps * sessions * width, d_local)
    picked, x_all = lax.optimization_barrier((pick(slot_from, held), x_all))
    pieces, masks = [picked], [0]
    for bit in reversed(range(beams.bit_length() - 1)):
        pieces = pieces + [partner_2(piece, "beam", bit) for piece in pieces]
        masks = masks + [mask ^ (1 << bit) for mask in masks]

    part, part_bc = project(x_all, w_inner, w_bc)
    part_dt = jnp.dot(x_all, w_dt, preferred_element_type=F32)
    rows = steps * sessions * width
    part_dt = jnp.pad(part_dt, ((0, rows), (0, -heads_local % 128)))
    part = jnp.concatenate([part, part_bc, part_dt], axis=1)
    whole = exchange(
        part.reshape(beams, 2 * rows // beams, part.shape[1]), "beam", True, 0, "sum_projections"
    ).reshape(part.shape)
    inner = whole[:, :channels]
    bc_new = whole[:, channels : channels + bc_local]
    dt_raw = whole[:rows, channels + bc_local : channels + bc_local + heads_local]
    gate_in, x_new = inner[:rows], inner[rows:]
    fresh = jnp.concatenate([x_new, bc_new[:rows], bc_new[rows:]], axis=1)
    wide = fresh.shape[1]
    fresh = fresh.reshape(steps, sessions, width, wide).transpose(1, 0, 2, 3)
    fresh = fresh.reshape(sessions, tokens, wide)
    source = jnp.concatenate([conv_held, fresh], axis=1)

    last = history[-1]
    taps = jnp.stack(
        [entry[:, :, step : step + tap_count] for step, entry in enumerate(history)], axis=1
    ).reshape(sessions, tokens, tap_count)
    mixed = 0.0
    for tap in range(tap_count):
        taken = jnp.einsum(
            "smi,sic->smc",
            onehot(taps[:, :, tap], sources, BF16),
            source,
            preferred_element_type=F32,
        )
        mixed = mixed + conv_w[tap].astype(F32) * taken
    conv = jax.nn.silu(mixed).astype(BF16)
    x_conv = conv[:, :, :channels]
    bc_conv = conv[:, :, channels:].reshape(sessions, tokens, 2, bc_local)
    for bit_number in range(group_span.bit_length() - 1):
        partner = partner_2(bc_conv, "row", bit_number)
        upper = jnp.bitwise_and(jnp.right_shift(row_index, bit_number), 1) == 1
        bc_conv = jnp.where(
            upper,
            jnp.concatenate([partner, bc_conv], axis=3),
            jnp.concatenate([bc_conv, partner], axis=3),
        )
    b_in, c_out = bc_conv[:, :, 0], bc_conv[:, :, 1]
    own_last = lax.dynamic_slice_in_dim(last, beam_index * local_beams, local_beams, 1)
    final_taps = onehot(own_last[:, :, steps : steps + tap_count - 1], sources, BF16)
    conv_final = jnp.einsum(
        "sbki,sic->sbkc", final_taps, source, preferred_element_type=F32
    ).astype(BF16)

    first = jnp.stack([entry[:, :, 0] for entry in history], axis=1).reshape(sessions, tokens)
    own_ids = beam_index * local_beams + jnp.arange(local_beams, dtype=jnp.int32)
    mine = first[:, None, :] == own_ids[None, :, None]
    c_masked = jnp.where(mine[..., None], c_out[:, None], 0).astype(BF16)
    from_held = read_held(c_masked.reshape(held_count, tokens, size), held, sessions)
    from_held = exchange(
        from_held.astype(BF16).reshape(beams, sessions * tokens // beams, channels),
        "beam",
        True,
        1,
        "sum_reads",
    )
    from_held = from_held.reshape(sessions, tokens, channels).astype(F32)

    step_size = jax.nn.softplus(dt_raw.astype(F32) + dt_bias)
    decay = jnp.exp(-jnp.exp(a_log) * step_size)
    step_size = step_size.reshape(steps, sessions, width, heads_local)
    decay = decay.reshape(steps, sessions, width, heads_local)
    factors = jnp.ones((sessions, width, 1, heads_local), F32)
    all_factors = []
    for step in range(steps):
        select = parents[step][:, :, None] == jnp.arange(width, dtype=jnp.int32)
        factors = jnp.concatenate(
            [
                decay[step][:, :, None] * choose(select, factors),
                step_size[step][:, :, None],
            ],
            axis=2,
        )
        short = steps - 1 - step
        all_factors.append(jnp.pad(factors, ((0, 0), (0, 0), (0, short), (0, 0))))
    all_factors = jnp.stack(all_factors, axis=1).reshape(
        sessions, tokens, steps + 1, heads_local
    )
    spread = jnp.repeat(jnp.eye(heads_local, dtype=F32), head_dim, axis=1)

    score = jnp.einsum("smn,sin->smi", c_out, b_in, preferred_element_type=F32)
    base = (tap_count - 1) * width
    read = from_held * jnp.dot(
        all_factors[:, :, 0], spread, precision=lax.Precision.HIGHEST
    ) + x_conv.astype(F32) * jnp.dot(d_skip[None, :], spread, precision=lax.Precision.HIGHEST)
    ancestors = [
        jnp.stack(
            [
                entry[:, :, tap_count - 1 + tau] - base if tau <= step else entry[:, :, 0] * 0 - 1
                for step, entry in enumerate(history)
            ],
            axis=1,
        ).reshape(sessions, tokens)
        for tau in range(steps)
    ]
    updates = []
    for tau in range(steps):
        select = onehot(ancestors[tau], tokens, F32)
        weight = jnp.sum(select * score, axis=2, keepdims=True) * all_factors[:, :, 1 + tau]
        taken = jnp.einsum(
            "smi,sic->smc", select.astype(BF16), x_conv, preferred_element_type=F32
        )
        read = read + jnp.dot(weight, spread, precision=lax.Precision.HIGHEST) * taken
        updates.append(taken)

    gate = gate_in.reshape(steps, sessions, width, channels).transpose(1, 0, 2, 3)
    gate = gate.reshape(sessions, tokens, channels).astype(F32)
    gated = read * jax.nn.silu(gate)
    square_sum = jnp.sum(gated * gated, axis=2, keepdims=True)
    if group_span > 1:
        group_index = row_index * heads_local // group_heads
        mask = (jnp.arange(GROUPS, dtype=jnp.int32) == group_index).astype(F32)
        totals = lax.psum(square_sum * mask, "row")
        square_sum = jnp.sum(totals * mask, axis=2, keepdims=True)
    mean_sq = square_sum / (group_heads * head_dim)
    normed = (gated * lax.rsqrt(mean_sq + EPS) * norm_gain).astype(BF16)
    normed = normed.reshape(sessions, steps, width, channels).transpose(1, 0, 2, 3)
    out = jnp.dot(normed.reshape(rows, channels), w_out, preferred_element_type=F32)
    row_count = lax.axis_size("row")
    out = out.astype(BF16).reshape(steps, row_count, sessions * width // row_count, -1)
    out = out.transpose(1, 0, 2, 3)
    block = out.shape[1:]
    layer_out = exchange(out.reshape(row_count, 16, -1), "row", False, 2, "sum_outputs")
    layer_out = layer_out.reshape(block)

    def own(values):
        return lax.dynamic_slice_in_dim(values, beam_index * local_beams, local_beams, 1)

    def own_rows(values):
        return own(values.reshape((sessions, steps, width) + values.shape[2:])[:, -1])

    own_factors = jnp.dot(
        own_rows(all_factors), spread, precision=lax.Precision.HIGHEST
    )
    update = jnp.stack([own_rows(taken) for taken in updates], axis=2) * own_factors[:, :, 1:]
    state_scale = own_factors[:, :, :1]
    high, low = split(update, 2)
    left = jnp.concatenate([high, low] + split(state_scale, 3), axis=2)
    own_tau = jnp.stack([own_rows(ids) for ids in ancestors], axis=2)
    b_last = jnp.einsum(
        "sbti,sin->sbtn", onehot(own_tau, tokens, BF16), b_in, preferred_element_type=F32
    ).astype(BF16)
    terms = -left.shape[2] % 16
    left = jnp.pad(left, ((0, 0), (0, 0), (0, terms), (0, 0)))
    ones = jnp.ones((sessions, local_beams, 3, size), BF16)
    right = jnp.concatenate(
        [
            jnp.pad(jnp.concatenate([b_last, b_last], axis=2), ((0, 0), (0, 0), (0, 0), (0, size))),
            jnp.pad(ones, ((0, 0), (0, 0), (0, 0), (size, 0))),
        ],
        axis=2,
    )
    right = jnp.pad(right, ((0, 0), (0, 0), (0, terms), (0, 0)))
    ancestor = own_last[:, :, 0]
    place = jnp.arange(sessions, dtype=jnp.int32)[:, None] * local_beams + ancestor % local_beams
    owner = ancestor // local_beams
    flat = (owner * held_count + place).reshape(-1)
    slot = jnp.sum(onehot(flat, beams * held_count, jnp.int32) * rank.reshape(-1), axis=-1)
    distance = jnp.bitwise_xor(owner.reshape(-1), beam_index)
    which = sum(jnp.where(distance == mask, piece, 0) for piece, mask in enumerate(masks))
    order = jnp.arange(held_count, dtype=jnp.int32)
    uses = which[None, :] == jnp.arange(beams, dtype=jnp.int32)[:, None]
    seen = uses[:, None, :] & (order[None, :] <= order[:, None])[None]
    latest = jnp.max(jnp.where(seen, order, -1), axis=2)
    where = jnp.sum(onehot(latest, held_count, jnp.int32) * slot, axis=-1)
    ssm_final = final_state(
        which.astype(jnp.int32),
        where.astype(jnp.int32),
        left.reshape((held_count,) + left.shape[2:]),
        right.reshape((held_count,) + right.shape[2:]),
        pieces,
    )
    return layer_out, ssm_final, conv_final


def local(
    x_in,
    w_inner,
    w_bc,
    w_dt,
    conv_x_w,
    conv_bc_w,
    dt_bias,
    a_log,
    d_skip,
    norm_gain,
    w_out,
    ssm_state,
    conv_x_state,
    conv_bc_state,
    parents,
):
    steps, sessions, width, _ = x_in.shape
    beams = lax.axis_size("beam")
    _, local_beams, heads_local, head_dim, size = ssm_state.shape
    channels = heads_local * head_dim
    tap_count = conv_x_w.shape[0]
    held_count = sessions * local_beams

    own = jnp.arange(width, dtype=jnp.int32)
    entry = jnp.stack([tap * width + own for tap in range(tap_count - 1)], axis=1)
    entry = jnp.broadcast_to(entry, (sessions, width, tap_count - 1))
    history = []
    for step in range(steps):
        select = parents[step][:, :, None] == own
        column = jnp.broadcast_to((tap_count - 1 + step) * width + own, (sessions, width))
        entry = jnp.concatenate([choose(select, entry), column[:, :, None]], axis=2)
        entry = entry.astype(jnp.int32)
        history.append(entry)
    needed = jnp.any(history[-1][:, :, :1] == own, axis=1)
    needed = needed.reshape(sessions, beams, local_beams).transpose(1, 0, 2)
    needed = needed.reshape(beams, held_count)
    ids = jnp.arange(held_count, dtype=jnp.int32)
    before = (ids[None, :] < ids[:, None])[None]
    rank = jnp.sum(jnp.where(before & needed[:, None, :], 1, 0), axis=2).astype(jnp.int32)
    most = jnp.max(jnp.sum(needed.astype(jnp.int32), axis=1))

    taps = jnp.transpose(conv_x_state, (0, 1, 4, 2, 3)).reshape(
        sessions, local_beams, tap_count - 1, channels
    )
    taps_bc = conv_bc_state.reshape(sessions, local_beams, tap_count - 1, -1)
    conv_held = lax.all_gather(
        jnp.concatenate([taps, taps_bc], axis=3), "beam", axis=1, tiled=True
    )
    conv_held = conv_held.transpose(0, 2, 1, 3).reshape(sessions, (tap_count - 1) * width, -1)
    conv_w = jnp.concatenate([conv_x_w, conv_bc_w.reshape(tap_count, -1)], axis=1)

    levels = [level for level in (3, 4, 5) if level < held_count] + [held_count]
    chosen = sum((most > level).astype(jnp.int32) for level in levels[:-1])
    layer_out, ssm_final, conv_final = lax.switch(
        chosen,
        [functools.partial(run, level) for level in levels],
        x_in,
        w_inner,
        w_bc,
        w_dt,
        conv_w,
        dt_bias,
        a_log,
        d_skip,
        norm_gain,
        w_out,
        ssm_state.reshape(held_count, channels, size),
        conv_held,
        history,
        needed,
        rank,
        parents,
    )
    conv_x_final = conv_final[..., :channels].reshape(
        sessions, local_beams, tap_count - 1, heads_local, head_dim
    )
    return (
        layer_out,
        ssm_final.reshape(ssm_state.shape),
        jnp.transpose(conv_x_final, (0, 1, 3, 4, 2)),
        conv_final[..., channels:].reshape(conv_bc_state.shape),
    )


def solution(mesh):
    placed = (
        P(None, None, None, "beam"),
        P("beam", None, "row"),
        P("beam", None, "row"),
        P("beam", "row"),
        P(None, "row"),
        P(None, None, "row"),
        P("row"),
        P("row"),
        P("row"),
        P("row"),
        P("row", "beam"),
        P(None, "beam", "row", None, None),
        P(None, "beam", "row", None, None),
        P(None, "beam", None, None, "row"),
        P(),
    )
    return jax.shard_map(
        local,
        mesh=mesh,
        in_specs=placed,
        out_specs=(
            P(None, "row", "beam"),
            P(None, "beam", "row", None, None),
            P(None, "beam", "row", None, None),
            P(None, "beam", None, None, "row"),
        ),
        check_vma=False,
    )
```

```python
import functools

import jax
import jax.numpy as jnp
from jax import lax
from jax.experimental import pallas as pl
from jax.experimental.pallas import tpu as pltpu
from jax.sharding import PartitionSpec as P

HEADS = 256
GROUPS = 8
EPS = 1e-05
MIB = 1 << 20
F32 = jnp.float32
BF16 = jnp.bfloat16


def partner_2(shard, axis, stride):
    return lax.ppermute(shard, axis, [(i, i ^ 1 << stride) for i in range(lax.axis_size(axis))])


def project_kernel(x_ref, w_ref, bc_ref, out_ref, out_bc_ref):
    tokens, depth = x_ref.shape
    row = lax.broadcasted_iota(jnp.int32, (depth, 2 * depth), 0)
    col = lax.broadcasted_iota(jnp.int32, (depth, 2 * depth), 1)
    x = x_ref[...]
    first = jnp.dot(x, (col == 2 * row).astype(BF16), preferred_element_type=F32).astype(BF16)
    second = jnp.dot(x, (col == 2 * row + 1).astype(BF16), preferred_element_type=F32).astype(BF16)
    spread = jnp.concatenate([first, second], axis=0)

    @pl.when(pl.program_id(0) == 0)
    def _():
        out_ref[...] = jnp.zeros_like(out_ref)
        out_bc_ref[...] = jnp.zeros_like(out_bc_ref)

    w = w_ref[...].reshape(2 * depth, w_ref.shape[2])
    bc = bc_ref[...].reshape(2 * depth, bc_ref.shape[2])
    out_ref[...] += jnp.dot(spread, w, preferred_element_type=F32)
    out_bc_ref[...] += jnp.dot(spread, bc, preferred_element_type=F32)


def project(x, w, w_bc):
    tokens, width = x.shape
    depth = 256
    columns, columns_bc = w.shape[2], w_bc.shape[2]
    return pl.pallas_call(
        project_kernel,
        grid=(width // depth,),
        in_specs=[
            pl.BlockSpec((tokens, depth), lambda i: (0, i)),
            pl.BlockSpec((depth, 2, columns), lambda i: (i, 0, 0)),
            pl.BlockSpec((depth, 2, columns_bc), lambda i: (i, 0, 0)),
        ],
        out_specs=[
            pl.BlockSpec((2 * tokens, columns), lambda i: (0, 0)),
            pl.BlockSpec((2 * tokens, columns_bc), lambda i: (0, 0)),
        ],
        out_shape=[
            jax.ShapeDtypeStruct((2 * tokens, columns), F32),
            jax.ShapeDtypeStruct((2 * tokens, columns_bc), F32),
        ],
        compiler_params=pltpu.CompilerParams(vmem_limit_bytes=40 * MIB),
        cost_estimate=pl.CostEstimate(
            flops=8 * tokens * width * columns,
            bytes_accessed=4 * width * columns,
            transcendentals=0,
        ),
        name="project",
    )(x, w, w_bc)


def pick_kernel(where_ref, held_ref, out_ref):
    out_ref[...] = held_ref[...]


def pick(where, held):
    count = where.shape[0]
    _, rows, columns = held.shape
    return pl.pallas_call(
        pick_kernel,
        grid_spec=pltpu.PrefetchScalarGridSpec(
            num_scalar_prefetch=1,
            grid=(count,),
            in_specs=[pl.BlockSpec((1, rows, columns), lambda i, where: (where[i], 0, 0))],
            out_specs=pl.BlockSpec((1, rows, columns), lambda i, where: (i, 0, 0)),
        ),
        out_shape=jax.ShapeDtypeStruct((count, rows, columns), held.dtype),
        compiler_params=pltpu.CompilerParams(vmem_limit_bytes=16 * MIB),
        name="pick",
    )(where, held)


def read_kernel(c_ref, held_ref, out_ref):
    part = lax.dot_general(
        c_ref[0], held_ref[0], (((1,), (1,)), ((), ())), preferred_element_type=F32
    )

    @pl.when(pl.program_id(1) == 0)
    def _():
        out_ref[0] = part

    @pl.when(pl.program_id(1) > 0)
    def _():
        out_ref[0] += part


def read_held(c_masked, held, sessions):
    blocks, tokens, size = c_masked.shape
    rows = held.shape[1]
    beams = blocks // sessions
    return pl.pallas_call(
        read_kernel,
        grid=(sessions, beams),
        in_specs=[
            pl.BlockSpec((1, tokens, size), lambda s, j: (s * beams + j, 0, 0)),
            pl.BlockSpec((1, rows, size), lambda s, j: (s * beams + j, 0, 0)),
        ],
        out_specs=pl.BlockSpec((1, tokens, rows), lambda s, j: (s, 0, 0)),
        out_shape=jax.ShapeDtypeStruct((sessions, tokens, rows), F32),
        compiler_params=pltpu.CompilerParams(vmem_limit_bytes=16 * MIB),
        cost_estimate=pl.CostEstimate(
            flops=2 * blocks * tokens * size * rows,
            bytes_accessed=2 * blocks * rows * size,
            transcendentals=0,
        ),
        name="read_held",
    )(c_masked, held)


def final_kernel(count, which_ref, where_ref, left_ref, right_ref, *refs):
    held_refs, out_ref = refs[:-1], refs[-1]
    size = out_ref.shape[2]
    both = lax.dot_general(
        left_ref[0], right_ref[0], (((0,), (0,)), ((), ())), preferred_element_type=F32
    )
    which = which_ref[pl.program_id(0)]
    for piece, held_ref in enumerate(held_refs):

        @pl.when(which == piece)
        def _(held_ref=held_ref):
            state = both[:, size:] * held_ref[0].astype(F32) + both[:, :size]
            out_ref[0] = state.astype(out_ref.dtype)


def final_state(which, where, left, right, pieces):
    count, terms, rows = left.shape
    size = pieces[0].shape[2]
    chunk = min(rows, 1024)
    chunks = rows // chunk

    def place(piece, i, k, which, where):
        block = jnp.where(which[i] == piece, k, chunks - 1)
        return where[piece * count + i], block, 0

    return pl.pallas_call(
        functools.partial(final_kernel, count),
        grid_spec=pltpu.PrefetchScalarGridSpec(
            num_scalar_prefetch=2,
            grid=(count, chunks),
            in_specs=[
                pl.BlockSpec((1, terms, chunk), lambda i, k, which, where: (i, 0, k)),
                pl.BlockSpec((1, terms, 2 * size), lambda i, k, which, where: (i, 0, 0)),
            ]
            + [
                pl.BlockSpec((1, chunk, size), functools.partial(place, piece))
                for piece in range(len(pieces))
            ],
            out_specs=pl.BlockSpec((1, chunk, size), lambda i, k, which, where: (i, k, 0)),
        ),
        out_shape=jax.ShapeDtypeStruct((count, rows, size), BF16),
        compiler_params=pltpu.CompilerParams(vmem_limit_bytes=32 * MIB),
        name="final_state",
    )(which, where.reshape(-1), left, right, *pieces)


def exchange_kernel(axis, count, gather, x_ref, out_ref, got, done, *sems):
    me = lax.axis_index(axis)
    peers = [lax.rem(me + hop, count) for hop in range(1, count)]
    barrier = pltpu.get_barrier_semaphore()
    for peer in peers:
        pl.semaphore_signal(
            barrier, inc=1, device_id={axis: peer}, device_id_type=pl.DeviceIdType.MESH
        )
    pl.semaphore_wait(barrier, count - 1)

    def send(src, dst, hop, sent, landed):
        copy = pltpu.make_async_remote_copy(
            src_ref=src,
            dst_ref=dst,
            send_sem=sent.at[hop],
            recv_sem=landed.at[hop],
            device_id={axis: peers[hop]},
            device_id_type=pl.DeviceIdType.MESH,
        )
        copy.start()
        return copy

    copies = [
        send(x_ref.at[peer], got.at[hop], hop, sems[0], sems[1]) for hop, peer in enumerate(peers)
    ]
    total = x_ref[me].astype(F32)
    for hop, copy in enumerate(copies):
        copy.wait()
        total = total + got[hop].astype(F32)
    if not gather:
        out_ref[...] = total.astype(out_ref.dtype)
        return
    done[me] = total.astype(done.dtype)
    copies = [send(done.at[me], done.at[me], hop, sems[2], sems[3]) for hop in range(count - 1)]
    for copy in copies:
        copy.wait()
    out_ref[...] = done[...]


def exchange(x, axis, gather, collective_id, name):
    count, rows, columns = x.shape
    shape = (count, rows, columns) if gather else (rows, columns)
    sems = [pltpu.SemaphoreType.DMA((count - 1,)) for _ in range(4)]
    return pl.pallas_call(
        functools.partial(exchange_kernel, axis, count, gather),
        out_shape=jax.ShapeDtypeStruct(shape, BF16),
        in_specs=[pl.BlockSpec(memory_space=pltpu.VMEM)],
        out_specs=pl.BlockSpec(memory_space=pltpu.VMEM),
        scratch_shapes=[
            pltpu.VMEM((count - 1, rows, columns), x.dtype),
            pltpu.VMEM((count, rows, columns) if gather else (1, 16, 128), BF16),
        ]
        + sems,
        compiler_params=pltpu.CompilerParams(
            collective_id=collective_id, has_side_effects=True, vmem_limit_bytes=32 * MIB
        ),
        name=name,
    )(x)


def split(value, pieces):
    out = []
    for _ in range(pieces):
        piece = value.astype(BF16)
        out.append(piece)
        value = value - piece.astype(F32)
    return out


def onehot(index, size, dtype):
    return (index[..., None] == jnp.arange(size, dtype=jnp.int32)).astype(dtype)


def choose(selector, values):
    extra = values.ndim - 2
    sel = selector.reshape(selector.shape + (1,) * extra)
    return jnp.sum(jnp.where(sel, values[:, None], 0), axis=2)


def run(
    slots_per_device,
    x_in,
    w_inner,
    w_bc,
    w_dt,
    conv_w,
    dt_bias,
    a_log,
    d_skip,
    norm_gain,
    w_out,
    held,
    conv_held,
    history,
    needed,
    rank,
    parents,
):
    beam_index = lax.axis_index("beam")
    row_index = lax.axis_index("row")
    steps, sessions, width, d_local = x_in.shape
    beams = lax.axis_size("beam")
    local_beams = width // beams
    held_count, channels, size = held.shape
    heads_local = w_dt.shape[1]
    head_dim = channels // heads_local
    tap_count = conv_w.shape[0]
    group_heads = HEADS // GROUPS
    group_span = lax.axis_size("row") // GROUPS
    bc_local = w_bc.shape[2]
    sources = (tap_count - 1 + steps) * width
    tokens = steps * width

    own_needed = lax.dynamic_index_in_dim(needed, beam_index, 0, keepdims=False)
    own_rank = lax.dynamic_index_in_dim(rank, beam_index, 0, keepdims=False)
    slot_ids = jnp.arange(slots_per_device, dtype=jnp.int32)
    in_slot = own_needed[None, :] & (own_rank[None, :] == slot_ids[:, None])
    slot_from = jnp.sum(
        jnp.where(in_slot, jnp.arange(held_count, dtype=jnp.int32)[None, :], 0), axis=1
    ).astype(jnp.int32)
    x_all = x_in.reshape(steps * sessions * width, d_local)
    cuts = [0, 1, 2, slots_per_device]
    picked = [pick(slot_from[low:high], held) for low, high in zip(cuts, cuts[1:])]
    picked, x_all = lax.optimization_barrier((picked, x_all))
    pieces, masks, starts = [], [], []

    top = beams.bit_length() - 2
    arrived = []

    def spread_out(part, piece, mask):
        parts, part_masks = [piece], [mask]
        for bit in reversed(range(top)):
            parts = parts + [partner_2(entry, "beam", bit) for entry in parts]
            part_masks = part_masks + [entry ^ (1 << bit) for entry in part_masks]
        pieces.extend(parts)
        masks.extend(part_masks)
        starts.extend([part] * len(parts))

    def send_round(part):
        arrived.append(partner_2(picked[part], "beam", top))
        spread_out(part, picked[part], 0)

    send_round(0)

    part, part_bc = project(x_all, w_inner, w_bc)
    part_dt = jnp.dot(x_all, w_dt, preferred_element_type=F32)
    rows = steps * sessions * width
    part_dt = jnp.pad(part_dt, ((0, rows), (0, -heads_local % 128)))
    part = jnp.concatenate([part, part_bc, part_dt], axis=1)
    whole = exchange(
        part.reshape(beams, 2 * rows // beams, part.shape[1]), "beam", True, 0, "sum_projections"
    ).reshape(part.shape)
    picked[1], whole = lax.optimization_barrier((picked[1], whole))
    send_round(1)
    inner = whole[:, :channels]
    bc_new = whole[:, channels : channels + bc_local]
    dt_raw = whole[:rows, channels + bc_local : channels + bc_local + heads_local]
    gate_in, x_new = inner[:rows], inner[rows:]
    fresh = jnp.concatenate([x_new, bc_new[:rows], bc_new[rows:]], axis=1)
    wide = fresh.shape[1]
    fresh = fresh.reshape(steps, sessions, width, wide).transpose(1, 0, 2, 3)
    fresh = fresh.reshape(sessions, tokens, wide)
    source = jnp.concatenate([conv_held, fresh], axis=1)

    last = history[-1]
    taps = jnp.stack(
        [entry[:, :, step : step + tap_count] for step, entry in enumerate(history)], axis=1
    ).reshape(sessions, tokens, tap_count)
    mixed = 0.0
    for tap in range(tap_count):
        taken = jnp.einsum(
            "smi,sic->smc",
            onehot(taps[:, :, tap], sources, BF16),
            source,
            preferred_element_type=F32,
        )
        mixed = mixed + conv_w[tap].astype(F32) * taken
    conv = jax.nn.silu(mixed).astype(BF16)
    x_conv = conv[:, :, :channels]
    bc_conv = conv[:, :, channels:].reshape(sessions, tokens, 2, bc_local)
    for bit_number in range(group_span.bit_length() - 1):
        partner = partner_2(bc_conv, "row", bit_number)
        upper = jnp.bitwise_and(jnp.right_shift(row_index, bit_number), 1) == 1
        bc_conv = jnp.where(
            upper,
            jnp.concatenate([partner, bc_conv], axis=3),
            jnp.concatenate([bc_conv, partner], axis=3),
        )
    b_in, c_out = bc_conv[:, :, 0], bc_conv[:, :, 1]
    own_last = lax.dynamic_slice_in_dim(last, beam_index * local_beams, local_beams, 1)
    final_taps = onehot(own_last[:, :, steps : steps + tap_count - 1], sources, BF16)
    conv_final = jnp.einsum(
        "sbki,sic->sbkc", final_taps, source, preferred_element_type=F32
    ).astype(BF16)

    first = jnp.stack([entry[:, :, 0] for entry in history], axis=1).reshape(sessions, tokens)
    own_ids = beam_index * local_beams + jnp.arange(local_beams, dtype=jnp.int32)
    mine = first[:, None, :] == own_ids[None, :, None]
    c_masked = jnp.where(mine[..., None], c_out[:, None], 0).astype(BF16)
    from_held = read_held(c_masked.reshape(held_count, tokens, size), held, sessions)
    from_held = exchange(
        from_held.astype(BF16).reshape(beams, sessions * tokens // beams, channels),
        "beam",
        True,
        1,
        "sum_reads",
    )
    picked[2], from_held = lax.optimization_barrier((picked[2], from_held))
    send_round(2)
    from_held = from_held.reshape(sessions, tokens, channels).astype(F32)

    step_size = jax.nn.softplus(dt_raw.astype(F32) + dt_bias)
    decay = jnp.exp(-jnp.exp(a_log) * step_size)
    step_size = step_size.reshape(steps, sessions, width, heads_local)
    decay = decay.reshape(steps, sessions, width, heads_local)
    factors = jnp.ones((sessions, width, 1, heads_local), F32)
    all_factors = []
    for step in range(steps):
        select = parents[step][:, :, None] == jnp.arange(width, dtype=jnp.int32)
        factors = jnp.concatenate(
            [
                decay[step][:, :, None] * choose(select, factors),
                step_size[step][:, :, None],
            ],
            axis=2,
        )
        short = steps - 1 - step
        all_factors.append(jnp.pad(factors, ((0, 0), (0, 0), (0, short), (0, 0))))
    all_factors = jnp.stack(all_factors, axis=1).reshape(
        sessions, tokens, steps + 1, heads_local
    )
    spread = jnp.repeat(jnp.eye(heads_local, dtype=F32), head_dim, axis=1)

    score = jnp.einsum("smn,sin->smi", c_out, b_in, preferred_element_type=F32)
    base = (tap_count - 1) * width
    read = from_held * jnp.dot(
        all_factors[:, :, 0], spread, precision=lax.Precision.HIGHEST
    ) + x_conv.astype(F32) * jnp.dot(d_skip[None, :], spread, precision=lax.Precision.HIGHEST)
    ancestors = [
        jnp.stack(
            [
                entry[:, :, tap_count - 1 + tau] - base if tau <= step else entry[:, :, 0] * 0 - 1
                for step, entry in enumerate(history)
            ],
            axis=1,
        ).reshape(sessions, tokens)
        for tau in range(steps)
    ]
    updates = []
    for tau in range(steps):
        select = onehot(ancestors[tau], tokens, F32)
        weight = jnp.sum(select * score, axis=2, keepdims=True) * all_factors[:, :, 1 + tau]
        taken = jnp.einsum(
            "smi,sic->smc", select.astype(BF16), x_conv, preferred_element_type=F32
        )
        read = read + jnp.dot(weight, spread, precision=lax.Precision.HIGHEST) * taken
        updates.append(taken)

    gate = gate_in.reshape(steps, sessions, width, channels).transpose(1, 0, 2, 3)
    gate = gate.reshape(sessions, tokens, channels).astype(F32)
    gated = read * jax.nn.silu(gate)
    square_sum = jnp.sum(gated * gated, axis=2, keepdims=True)
    if group_span > 1:
        group_index = row_index * heads_local // group_heads
        mask = (jnp.arange(GROUPS, dtype=jnp.int32) == group_index).astype(F32)
        totals = lax.psum(square_sum * mask, "row")
        square_sum = jnp.sum(totals * mask, axis=2, keepdims=True)
    mean_sq = square_sum / (group_heads * head_dim)
    normed = (gated * lax.rsqrt(mean_sq + EPS) * norm_gain).astype(BF16)
    normed = normed.reshape(sessions, steps, width, channels).transpose(1, 0, 2, 3)
    out = jnp.dot(normed.reshape(rows, channels), w_out, preferred_element_type=F32)
    row_count = lax.axis_size("row")
    out = out.astype(BF16).reshape(steps, row_count, sessions * width // row_count, -1)
    out = out.transpose(1, 0, 2, 3)
    block = out.shape[1:]
    layer_out = exchange(out.reshape(row_count, 16, -1), "row", False, 2, "sum_outputs")
    layer_out = layer_out.reshape(block)
    arrived, layer_out = lax.optimization_barrier((arrived, layer_out))
    for part, piece in enumerate(arrived):
        spread_out(part, piece, 1 << top)

    def own(values):
        return lax.dynamic_slice_in_dim(values, beam_index * local_beams, local_beams, 1)

    def own_rows(values):
        return own(values.reshape((sessions, steps, width) + values.shape[2:])[:, -1])

    own_factors = jnp.dot(
        own_rows(all_factors), spread, precision=lax.Precision.HIGHEST
    )
    update = jnp.stack([own_rows(taken) for taken in updates], axis=2) * own_factors[:, :, 1:]
    state_scale = own_factors[:, :, :1]
    high, low = split(update, 2)
    left = jnp.concatenate([high, low] + split(state_scale, 3), axis=2)
    own_tau = jnp.stack([own_rows(ids) for ids in ancestors], axis=2)
    b_last = jnp.einsum(
        "sbti,sin->sbtn", onehot(own_tau, tokens, BF16), b_in, preferred_element_type=F32
    ).astype(BF16)
    terms = -left.shape[2] % 16
    left = jnp.pad(left, ((0, 0), (0, 0), (0, terms), (0, 0)))
    ones = jnp.ones((sessions, local_beams, 3, size), BF16)
    right = jnp.concatenate(
        [
            jnp.pad(jnp.concatenate([b_last, b_last], axis=2), ((0, 0), (0, 0), (0, 0), (0, size))),
            jnp.pad(ones, ((0, 0), (0, 0), (0, 0), (size, 0))),
        ],
        axis=2,
    )
    right = jnp.pad(right, ((0, 0), (0, 0), (0, terms), (0, 0)))
    ancestor = own_last[:, :, 0]
    place = jnp.arange(sessions, dtype=jnp.int32)[:, None] * local_beams + ancestor % local_beams
    owner = ancestor // local_beams
    flat = (owner * held_count + place).reshape(-1)
    slot = jnp.sum(onehot(flat, beams * held_count, jnp.int32) * rank.reshape(-1), axis=-1)
    distance = jnp.bitwise_xor(owner.reshape(-1), beam_index)
    part = sum((slot >= cut).astype(jnp.int32) for cut in cuts[1:-1])
    slot = slot - sum(jnp.where(part == index, cut, 0) for index, cut in enumerate(cuts[:-1]))
    which = sum(
        jnp.where((distance == mask) & (part == start), piece, 0)
        for piece, (mask, start) in enumerate(zip(masks, starts))
    )
    order = jnp.arange(held_count, dtype=jnp.int32)
    uses = which[None, :] == jnp.arange(len(pieces), dtype=jnp.int32)[:, None]
    seen = uses[:, None, :] & (order[None, :] <= order[:, None])[None]
    latest = jnp.max(jnp.where(seen, order, -1), axis=2)
    where = jnp.sum(onehot(latest, held_count, jnp.int32) * slot, axis=-1)
    ssm_final = final_state(
        which.astype(jnp.int32),
        where.astype(jnp.int32),
        left.reshape((held_count,) + left.shape[2:]),
        right.reshape((held_count,) + right.shape[2:]),
        pieces,
    )
    return layer_out, ssm_final, conv_final


def local(
    x_in,
    w_inner,
    w_bc,
    w_dt,
    conv_x_w,
    conv_bc_w,
    dt_bias,
    a_log,
    d_skip,
    norm_gain,
    w_out,
    ssm_state,
    conv_x_state,
    conv_bc_state,
    parents,
):
    steps, sessions, width, _ = x_in.shape
    beams = lax.axis_size("beam")
    _, local_beams, heads_local, head_dim, size = ssm_state.shape
    channels = heads_local * head_dim
    tap_count = conv_x_w.shape[0]
    held_count = sessions * local_beams

    own = jnp.arange(width, dtype=jnp.int32)
    entry = jnp.stack([tap * width + own for tap in range(tap_count - 1)], axis=1)
    entry = jnp.broadcast_to(entry, (sessions, width, tap_count - 1))
    history = []
    for step in range(steps):
        select = parents[step][:, :, None] == own
        column = jnp.broadcast_to((tap_count - 1 + step) * width + own, (sessions, width))
        entry = jnp.concatenate([choose(select, entry), column[:, :, None]], axis=2)
        entry = entry.astype(jnp.int32)
        history.append(entry)
    needed = jnp.any(history[-1][:, :, :1] == own, axis=1)
    needed = needed.reshape(sessions, beams, local_beams).transpose(1, 0, 2)
    needed = needed.reshape(beams, held_count)
    ids = jnp.arange(held_count, dtype=jnp.int32)
    before = (ids[None, :] < ids[:, None])[None]
    rank = jnp.sum(jnp.where(before & needed[:, None, :], 1, 0), axis=2).astype(jnp.int32)
    most = jnp.max(jnp.sum(needed.astype(jnp.int32), axis=1))

    taps = jnp.transpose(conv_x_state, (0, 1, 4, 2, 3)).reshape(
        sessions, local_beams, tap_count - 1, channels
    )
    taps_bc = conv_bc_state.reshape(sessions, local_beams, tap_count - 1, -1)
    conv_held = lax.all_gather(
        jnp.concatenate([taps, taps_bc], axis=3), "beam", axis=1, tiled=True
    )
    conv_held = conv_held.transpose(0, 2, 1, 3).reshape(sessions, (tap_count - 1) * width, -1)
    conv_w = jnp.concatenate([conv_x_w, conv_bc_w.reshape(tap_count, -1)], axis=1)

    levels = [level for level in (3, 4, 5) if level < held_count] + [held_count]
    chosen = sum((most > level).astype(jnp.int32) for level in levels[:-1])
    layer_out, ssm_final, conv_final = lax.switch(
        chosen,
        [functools.partial(run, level) for level in levels],
        x_in,
        w_inner,
        w_bc,
        w_dt,
        conv_w,
        dt_bias,
        a_log,
        d_skip,
        norm_gain,
        w_out,
        ssm_state.reshape(held_count, channels, size),
        conv_held,
        history,
        needed,
        rank,
        parents,
    )
    conv_x_final = conv_final[..., :channels].reshape(
        sessions, local_beams, tap_count - 1, heads_local, head_dim
    )
    return (
        layer_out,
        ssm_final.reshape(ssm_state.shape),
        jnp.transpose(conv_x_final, (0, 1, 3, 4, 2)),
        conv_final[..., channels:].reshape(conv_bc_state.shape),
    )


def solution(mesh):
    placed = (
        P(None, None, None, "beam"),
        P("beam", None, "row"),
        P("beam", None, "row"),
        P("beam", "row"),
        P(None, "row"),
        P(None, None, "row"),
        P("row"),
        P("row"),
        P("row"),
        P("row"),
        P("row", "beam"),
        P(None, "beam", "row", None, None),
        P(None, "beam", "row", None, None),
        P(None, "beam", None, None, "row"),
        P(),
    )
    return jax.shard_map(
        local,
        mesh=mesh,
        in_specs=placed,
        out_specs=(
            P(None, "row", "beam"),
            P(None, "beam", "row", None, None),
            P(None, "beam", "row", None, None),
            P(None, "beam", None, None, "row"),
        ),
        check_vma=False,
    )
```
